32 devices in a mesh: batch: 4 (over x, core), tensor: 8 (over z, y).
Axes of the slice: x: 2, y: 2, z: 4, core: 2. Of those that a mesh axis runs over, the one named last changes fastest.
Arguments:
- inputs: bfloat16 [4, 8, 32, 4096], P(None, 'batch', 'tensor'), may hold values from -6 to 6
- norm_gain: float32 [4096], replicated, may hold values from 0.5 to 1.5
- norm_bias: float32 [4096], replicated, may hold values from -3 to 3
- qkv_weight: bfloat16 [4096, 3, 4096], P(None, None, 'tensor'), may hold values from -0.09375 to 0.09375
- out_weight: bfloat16 [4096, 4096], P('tensor'), may hold values from -0.375 to 0.375
- in_weight: bfloat16 [4096, 8192], P(None, 'tensor'), may hold values from -0.09375 to 0.09375
- in_bias: float32 [8192], P('tensor'), may hold values from -3 to 3
- down_weight: bfloat16 [8192, 4096], P('tensor'), may hold values from -0.0625 to 0.0625
- down_bias: float32 [4096], replicated, may hold values from -3 to 3
- page_pool: bfloat16 [128, 2, 128, 4096], P('batch', None, None, 'tensor'), may hold values from -103 to 103
- old_cache: bfloat16 [8, 32, 2, 64, 4096], P('batch', None, None, None, 'tensor'), may hold values from -103 to 103, as said below
- page_table: int32 [32, 4], replicated, may hold values from 0 to 127, as said below
- prompt_length: int32 [32], replicated, may hold values from 1 to 512, 8192 in all
- parents: int32 [4, 8, 32], replicated, may hold values from 0 to 7
Outputs:
- outputs: float32 [4, 8, 32, 4096], P(None, 'batch', 'tensor')
The draws below stay inside these ranges and needn't reach their ends.
Inputs may be any that keep to these rules, and one draw needn't show every extreme that they name: `old_cache`: key and value entries of the beams' generated tokens. `page_table`: every pool page is named exactly once in the table. The pool is cut into as many equal blocks of consecutive pages as the batch axis has devices; request r names only pages of block r modulo that count.
All inputs are finite; a program needn't handle non-finite values.
Results may differ from the reference program's by a relative error of at most 0.034.
Values may be sent and summed in bfloat16 or wider, within the bound.
A program may use at most 256 MiB of HBM per device.

```python
import math
import jax
import jax.numpy as jnp
import numpy as np
from jax import lax

D = 4096
HEADS = 16
HDIM = 256
ROT = 64
FF = 8192
BEAMS = 8
REQ = 32
STEPS = 4
PAGE = 128
PPAGES = 4
GEN = 64
POOL = 128
N_BATCH = 4


def cache_entries(key, array_shape):
    return jnp.clip(jax.random.normal(jax.random.fold_in(key, 13), array_shape, jnp.float32), -4.0, 4.0)


def draw_page_pool(key, part):
    return cache_entries(key, (POOL, 2, PAGE, HEADS * HDIM)).astype(jnp.bfloat16)


def draw_old_cache(key, part):
    return cache_entries(key, (BEAMS, REQ, 2, GEN, HEADS * HDIM)).astype(jnp.bfloat16)


def draw_page_table(key, part):
    group_count = N_BATCH
    pages_each = POOL // group_count
    owned_requests = REQ // group_count
    group_keys = jax.random.split(jax.random.fold_in(key, 21), group_count)
    shuffled = jax.vmap(lambda single: jax.random.permutation(single, pages_each))(group_keys)
    local_table = shuffled.reshape(group_count, owned_requests, PPAGES)
    offsets = (jnp.arange(group_count) * pages_each)[:, None, None]
    placed = local_table + offsets
    return jnp.transpose(placed, (1, 0, 2)).reshape(REQ, PPAGES).astype(jnp.int32)


def set_ends(array, rng, smallest, largest):
    dims = array.shape
    place = [jax.random.randint(jax.random.fold_in(rng, axis), (), 0, dims[axis]) for axis in range(len(dims))]
    array = array.at[tuple(place)].set(smallest)
    longest = dims.index(max(dims))
    place[longest] = (place[longest] + 1) % dims[longest]
    return array.at[tuple(place)].set(largest)


def block_scale(rng, dims, cuts, least, high):
    def one(dim, shards_of):
        heights = jax.random.uniform(jax.random.fold_in(jax.random.fold_in(rng, 6), dim), (shards_of,), jnp.float32, least / len(cuts), high / len(cuts))
        return jnp.repeat(jnp.exp(heights), dims[dim] // shards_of).reshape((-1,) + (1,) * (len(dims) - dim - 1))

    level = one(*cuts[0])
    for cut in cuts[1:]:
        level = level * one(*cut)
    return level


def profile(amount, total, limit, slope):
    portions = [(1 << 20) // math.isqrt(grade ** slope) + 1 for grade in range(2, amount + 1)]
    spare, holding = total - limit - (amount - 1), [1] * (amount - 1)
    while spare > 0:
        candidates = [i for i in range(amount - 1) if holding[i] < limit]
        whole, left = sum([portions[i] for i in candidates]), spare
        for i in candidates:
            addition = min(limit - holding[i], max(1, left * portions[i] // whole), spare)
            holding[i] = holding[i] + addition
            spare = spare - addition
    return np.array([limit] + holding)


def ragged_sizes(key, count, total, limit, skew):
    if count == 2:
        one = jax.random.randint(key, (), max(1, total - limit), min(limit, total - 1) + 1)
        return jnp.stack([one, total - one])
    lengths = jnp.asarray(profile(count, total, limit, skew), jnp.int32)
    couples = (count - 1) // 2
    donor, receiver = lengths[1:1 + 2 * couples:2], lengths[2:2 + 2 * couples:2]
    slack = jnp.minimum(donor - 1, limit - receiver)
    moved = jax.random.randint(jax.random.fold_in(key, 1), (couples,), 0, 1 << 20) % (slack + 1)
    lengths = lengths.at[1:1 + 2 * couples:2].set(donor - moved).at[2:2 + 2 * couples:2].set(receiver + moved)
    return lengths[jax.random.permutation(jax.random.fold_in(key, 2), count)]


def bell_draw(own_key, dims, width, most, cuts=(), held_as=jnp.bfloat16):
    gain = block_scale(own_key, dims, cuts, -0.22, 0.18) if cuts else 1.0
    drawn = jax.random.normal(own_key, dims, jnp.float32) * width * gain
    return jnp.minimum(jnp.maximum(drawn, -most), most).astype(held_as)


def setup_inputs(seed: int = 0) -> dict:
    splits = jax.random.split(jax.random.key(seed), 15)
    return {
        "inputs": bell_draw(splits[0], (STEPS, BEAMS, REQ, D), 1.0, 6.0, ((1, 4), (2, 8))),
        "norm_gain": jnp.clip(1.0 + 0.1 * jax.random.normal(splits[1], (D,), jnp.float32), 0.5, 1.5),
        "norm_bias": bell_draw(splits[2], (D,), 0.5, 3.0, (), jnp.float32),
        "qkv_weight": bell_draw(splits[3], (D, 3, HEADS * HDIM), D ** -0.5, 0.09375, ((2, 8),)),
        "out_weight": bell_draw(splits[4], (HEADS * HDIM, D), HDIM ** -0.5, 0.375, ((0, 8),)),
        "in_weight": bell_draw(splits[5], (D, FF), D ** -0.5, 0.09375, ((1, 8),)),
        "in_bias": bell_draw(splits[6], (FF,), 0.5, 3.0, ((0, 8),), jnp.float32),
        "down_weight": bell_draw(splits[7], (FF, D), FF ** -0.5, 0.0625, ((0, 8),)),
        "down_bias": bell_draw(splits[8], (D,), 0.5, 3.0, (), jnp.float32),
        "page_pool": draw_page_pool(jax.random.fold_in(splits[14], 71), 0),
        "old_cache": draw_old_cache(jax.random.fold_in(splits[14], 71), 0),
        "page_table": draw_page_table(jax.random.fold_in(splits[14], 71), 0),
        "prompt_length": ragged_sizes(splits[12], REQ, REQ * PPAGES * PAGE // 2, PPAGES * PAGE, 2).astype(jnp.int32),
        "parents": set_ends(jax.random.randint(splits[13], (STEPS, BEAMS, REQ), 0, BEAMS), jax.random.fold_in(splits[13], 1), 0, BEAMS - 1).astype(jnp.int32),
    }


def normalize(row_block, norm_gain, norm_bias):
    widened = row_block.astype(jnp.float32)
    center = lax.optimization_barrier(jnp.mean(widened, axis=-1, keepdims=True))
    shifted = widened - center
    variance = lax.optimization_barrier(jnp.mean(shifted * shifted, axis=-1, keepdims=True))
    return shifted * lax.rsqrt(variance + 1e-05) * norm_gain + norm_bias

def rotate_heads(vectors, position):
    halves = vectors.reshape(vectors.shape[:-1] + (HDIM // 2, 2))
    doubled = 2 * jnp.arange(HDIM // 2)
    exponent = doubled.astype(jnp.float32) / ROT
    frequency = jnp.where(doubled < ROT, jnp.exp(-exponent * math.log(10000.0)), 0.0)
    angles = position[:, None] * frequency[None, :]
    cosine = jnp.cos(angles)[None, :, None, :]
    sine_part = jnp.sin(angles)[None, :, None, :]
    even_part = halves[..., 0]
    odd_part = halves[..., 1]
    turned = jnp.stack([even_part * cosine - odd_part * sine_part, odd_part * cosine + even_part * sine_part], axis=-1)
    return turned.reshape(vectors.shape)

def reference(inputs, norm_gain, norm_bias, qkv_weight, out_weight, in_weight, in_bias, down_weight, down_bias, page_pool, old_cache, page_table, prompt_length, parents):
    total_width = HEADS * HDIM
    cache_span = GEN + STEPS
    prompt_span = PPAGES * PAGE
    scale_factor = HDIM ** (-0.5)
    cache = jnp.concatenate([old_cache, jnp.zeros((BEAMS, REQ, 2, STEPS, total_width), jnp.bfloat16)], axis=3)
    prompt_valid = jnp.arange(prompt_span)[None, :] < prompt_length[:, None]
    request_ids = jnp.arange(REQ).astype(jnp.int32)
    outputs = []
    for step_index in range(STEPS):
        current = inputs[step_index]
        normed = normalize(current, norm_gain, norm_bias).astype(jnp.bfloat16)
        flat_rows = normed.reshape(BEAMS * REQ, D)
        projected = jnp.dot(flat_rows, qkv_weight.reshape(D, 3 * total_width), preferred_element_type=jnp.float32)
        projected = projected.reshape(BEAMS, REQ, 3, HEADS, HDIM)
        position = (prompt_length + GEN + step_index).astype(jnp.float32)
        queries = rotate_heads(projected[:, :, 0], position).astype(jnp.bfloat16)
        fresh_keys = rotate_heads(projected[:, :, 1], position).astype(jnp.bfloat16)
        fresh_values = projected[:, :, 2].astype(jnp.bfloat16)
        cache = cache[parents[step_index], request_ids[None, :]]
        new_entry = jnp.stack([fresh_keys.reshape(BEAMS, REQ, total_width), fresh_values.reshape(BEAMS, REQ, total_width)], axis=2)
        cache = cache.at[:, :, :, GEN + step_index].set(new_entry)
        live_mask = jnp.arange(cache_span) <= GEN + step_index

        def attend(request_id):
            query_rows = lax.dynamic_index_in_dim(queries, request_id, 1, keepdims=False).astype(jnp.float32)
            beam_cache = lax.dynamic_index_in_dim(cache, request_id, 1, keepdims=False)
            table_row = lax.dynamic_index_in_dim(page_table, request_id, 0, keepdims=False)
            valid_row = lax.dynamic_index_in_dim(prompt_valid, request_id, 0, keepdims=False)
            page_rows = page_pool[table_row]
            prompt_keys = page_rows[:, 0].reshape(prompt_span, HEADS, HDIM).astype(jnp.float32)
            prompt_values = page_rows[:, 1].reshape(prompt_span, HEADS, HDIM).astype(jnp.float32)
            own_keys = beam_cache[:, 0].reshape(BEAMS, cache_span, HEADS, HDIM).astype(jnp.float32)
            own_values = beam_cache[:, 1].reshape(BEAMS, cache_span, HEADS, HDIM).astype(jnp.float32)
            prompt_scores = jnp.einsum('bhd,thd->bht', query_rows, prompt_keys) * scale_factor
            own_scores = jnp.einsum('bhd,bthd->bht', query_rows, own_keys) * scale_factor
            prompt_scores = jnp.where(valid_row[None, None, :], prompt_scores, -jnp.inf)
            own_scores = jnp.where(live_mask[None, None, :], own_scores, -jnp.inf)
            peak = jnp.maximum(lax.optimization_barrier(jnp.max(prompt_scores, axis=-1)), lax.optimization_barrier(jnp.max(own_scores, axis=-1)))
            prompt_exp = jnp.exp(prompt_scores - peak[..., None])
            own_exp = jnp.exp(own_scores - peak[..., None])
            totals = lax.optimization_barrier(jnp.sum(prompt_exp, axis=-1)) + lax.optimization_barrier(jnp.sum(own_exp, axis=-1))
            prompt_round = lax.optimization_barrier(prompt_exp.astype(jnp.bfloat16)).astype(jnp.float32)
            own_round = lax.optimization_barrier(own_exp.astype(jnp.bfloat16)).astype(jnp.float32)
            mixture = jnp.einsum('bht,thd->bhd', prompt_round, prompt_values) + jnp.einsum('bht,bthd->bhd', own_round, own_values)
            return (mixture / totals[..., None]).reshape(BEAMS, total_width)
        attended = lax.map(attend, request_ids)
        attention = jnp.transpose(attended, (1, 0, 2)).astype(jnp.bfloat16)
        hidden = jax.nn.gelu(jnp.dot(flat_rows, in_weight, preferred_element_type=jnp.float32) + in_bias, approximate=True).astype(jnp.bfloat16)
        attn_update = jnp.dot(attention.reshape(BEAMS * REQ, total_width), out_weight, preferred_element_type=jnp.float32)
        mlp_update = jnp.dot(hidden, down_weight, preferred_element_type=jnp.float32)
        result = current.astype(jnp.float32) + (attn_update + mlp_update).reshape(BEAMS, REQ, D) + down_bias
        outputs.append(result.astype(jnp.float32))
    return jnp.stack(outputs, axis=0)
```

```python
import math

import jax
import jax.numpy as jnp
from jax import lax
from jax.experimental import pallas as pl
from jax.experimental.pallas import tpu as pltpu
from jax.sharding import PartitionSpec as P

HDIM = 256
ROT = 64
BEAMS = 8
STEPS = 4


NEG_FILL = -1e30


def partner(value, axis, bit):
    return lax.ppermute(value, axis, [(i, i ^ 1 << bit) for i in range(lax.axis_size(axis))])


def joined_2(part, axis, combine):
    gathered = jax.tree.map(lambda a: lax.all_gather(a, axis), part)

    def take(source):
        return jax.tree.map(lambda a: lax.dynamic_index_in_dim(a, source, 0, False), gathered)

    return lax.fori_loop(
        1, lax.axis_size(axis), lambda source, state: combine(state, take(source)), take(0)
    )


def normalize(row_block, norm_gain, norm_bias):
    widened = row_block.astype(jnp.float32)
    center = jnp.mean(widened, axis=-1, keepdims=True)
    shifted = widened - center
    variance = jnp.mean(shifted * shifted, axis=-1, keepdims=True)
    return shifted * lax.rsqrt(variance + 1e-05) * norm_gain + norm_bias


def rotate_local(vectors, position, first_column):
    half_count = vectors.shape[-1] // 2
    doubled = (first_column + 2 * jnp.arange(half_count)) % HDIM
    exponent = doubled.astype(jnp.float32) / ROT
    frequency = jnp.where(doubled < ROT, jnp.exp(-exponent * math.log(10000.0)), 0.0)
    angles = position[:, None] * frequency[None, :]
    cosine = jnp.cos(angles)[None]
    sine_part = jnp.sin(angles)[None]
    halves = vectors.reshape(vectors.shape[:-1] + (half_count, 2))
    even_part = halves[..., 0]
    odd_part = halves[..., 1]
    turned = jnp.stack(
        [even_part * cosine - odd_part * sine_part, odd_part * cosine + even_part * sine_part],
        axis=-1,
    )
    return turned.reshape(vectors.shape)


def combine(earlier, later):
    peak_one, total_one, mixture_one = earlier
    peak_two, total_two, mixture_two = later
    peak = jnp.maximum(peak_one, peak_two)
    factor_one = jnp.exp(peak_one - peak)
    factor_two = jnp.exp(peak_two - peak)
    return (
        peak,
        total_one * factor_one + total_two * factor_two,
        mixture_one * factor_one[..., None] + mixture_two * factor_two[..., None],
    )


def partial_softmax(scores, allowed):
    masked = jnp.where(allowed, scores, NEG_FILL)
    peak = jnp.max(masked, axis=-1)
    weights = jnp.where(allowed, jnp.exp(masked - peak[..., None]), 0.0)
    return (peak, jnp.sum(weights, axis=-1), weights.astype(jnp.bfloat16))


def place_block(values, slot, slot_count, axis, fill_value):
    hit_shape = [1] * (values.ndim + 1)
    hit_shape[axis] = slot_count
    hits = (jnp.arange(slot_count) == slot).reshape(hit_shape)
    return jnp.where(hits, jnp.expand_dims(values, axis), fill_value)


def head_sum(prompt_scores, chain_scores, spread):
    for bit_index in range(spread.bit_length() - 1):
        other_prompt, other_chain = partner((prompt_scores, chain_scores), "tensor", bit_index)
        prompt_scores = prompt_scores + other_prompt
        chain_scores = chain_scores + other_chain
    return (prompt_scores, chain_scores)


def stepwise(
    inputs,
    norm_gain,
    norm_bias,
    qkv_weight,
    out_weight,
    in_weight,
    in_bias,
    down_weight,
    down_bias,
    page_pool,
    old_cache,
    page_table,
    prompt_length,
    parents,
):
    batch_index = lax.axis_index("batch")
    tensor_index = lax.axis_index("tensor")
    groups = lax.axis_size("batch")
    beam_dev = inputs.shape[1]
    model_width = inputs.shape[3]
    columns = qkv_weight.shape[2]
    requests = page_table.shape[0]
    history = old_cache.shape[3]
    prompt_span = page_table.shape[1] * page_pool.shape[2]
    heads_dev = max(columns // HDIM, 1)
    head_part = min(columns, HDIM)
    spread = max(HDIM // columns, 1)
    scale_factor = HDIM ** (-0.5)
    qkv_flat = qkv_weight.reshape(model_width, 3 * columns)
    first_column = tensor_index * columns
    owners = batch_index * beam_dev + jnp.arange(beam_dev)
    old_keys = old_cache[:, :, 0].reshape(beam_dev, requests, history, heads_dev, head_part)
    old_values = old_cache[:, :, 1].reshape(beam_dev, requests, history, heads_dev, head_part)
    stored_keys = jnp.zeros((beam_dev, requests, STEPS, columns), jnp.bfloat16)
    stored_values = jnp.zeros((beam_dev, requests, STEPS, columns), jnp.bfloat16)
    beam_ids = jnp.broadcast_to(jnp.arange(BEAMS)[:, None], (BEAMS, requests))
    prompt_ok = jnp.arange(prompt_span)[None, :] < prompt_length[:, None]
    whole_pool = lax.all_gather(page_pool, "batch", axis=0, tiled=True)
    page_rows = whole_pool[page_table]
    count_rows = page_table.shape[0]
    prompt_keys = page_rows[:, :, 0].reshape(count_rows, prompt_span, heads_dev, head_part)
    prompt_values = page_rows[:, :, 1].reshape(count_rows, prompt_span, heads_dev, head_part)
    outputs = []
    for step_index in range(STEPS):
        current = inputs[step_index]
        normed = normalize(current, norm_gain, norm_bias).astype(jnp.bfloat16)
        gathered_rows = lax.all_gather(normed, "tensor", axis=1, tiled=True)
        attn_part = jnp.einsum(
            "brd,dc->brc", gathered_rows, qkv_flat, preferred_element_type=jnp.float32
        )
        ffn_part = jnp.einsum(
            "brd,dc->brc", gathered_rows, in_weight, preferred_element_type=jnp.float32
        )
        projected = jnp.concatenate([attn_part, ffn_part], axis=-1)
        position = (prompt_length + history + step_index).astype(jnp.float32)
        queries = rotate_local(projected[..., :columns], position, first_column).astype(
            jnp.bfloat16
        )
        fresh_keys = rotate_local(
            projected[..., columns : 2 * columns], position, first_column
        ).astype(jnp.bfloat16)
        fresh_values = projected[..., 2 * columns : 3 * columns].astype(jnp.bfloat16)
        hidden = jax.nn.gelu(projected[..., 3 * columns :] + in_bias, approximate=True).astype(
            jnp.bfloat16
        )
        stored_keys = stored_keys.at[:, :, step_index].set(fresh_keys)
        stored_values = stored_values.at[:, :, step_index].set(fresh_values)
        queries_all = lax.all_gather(queries, "batch", axis=0, tiled=True)
        query_heads = queries_all.reshape(BEAMS, requests, heads_dev, head_part)
        own_heads = queries.reshape(beam_dev, requests, heads_dev, head_part)
        ancestry = []
        lineage = beam_ids
        for back_step in range(step_index, -1, -1):
            ancestry.append(lineage)
            lineage = jnp.take_along_axis(parents[back_step], lineage, axis=0)
        unused_steps = [jnp.full_like(beam_ids, -1)] * (STEPS - 1 - step_index)
        ancestry_all = jnp.stack(ancestry[::-1] + unused_steps, axis=-1)
        stored_k = stored_keys.reshape(beam_dev, requests, STEPS, heads_dev, head_part)
        stored_v = stored_values.reshape(beam_dev, requests, STEPS, heads_dev, head_part)
        chain_scores = (
            jnp.concatenate(
                [
                    jnp.einsum(
                        "brnd,jrtnd->brnjt",
                        query_heads,
                        old_keys,
                        preferred_element_type=jnp.float32,
                    ),
                    jnp.einsum(
                        "brnd,jrtnd->brnjt",
                        query_heads,
                        stored_k,
                        preferred_element_type=jnp.float32,
                    ),
                ],
                axis=-1,
            )
            * scale_factor
        )
        old_ok = jnp.broadcast_to(
            (lineage[:, :, None] == owners[None, None, :])[:, :, :, None],
            (BEAMS, requests, beam_dev, history),
        )
        new_ok = ancestry_all[:, :, None, :] == owners[None, None, :, None]
        chain_ok = jnp.concatenate([old_ok, new_ok], axis=-1).reshape(BEAMS, requests, 1, -1)
        prompt_scores = (
            jnp.einsum(
                "brnd,rtnd->brnt", own_heads, prompt_keys, preferred_element_type=jnp.float32
            )
            * scale_factor
        )
        prompt_scores, chain_scores = head_sum(prompt_scores, chain_scores, spread)
        prompt_peak, prompt_total, prompt_weights = partial_softmax(
            prompt_scores, prompt_ok[None, :, None, :]
        )
        prompt_mix = jnp.einsum(
            "brnt,rtnd->brnd", prompt_weights, prompt_values, preferred_element_type=jnp.float32
        )
        peak_full = place_block(prompt_peak, batch_index, groups, 0, NEG_FILL).reshape(
            BEAMS, requests, heads_dev
        )
        total_full = place_block(prompt_total, batch_index, groups, 0, 0.0).reshape(
            BEAMS, requests, heads_dev
        )
        mix_full = place_block(prompt_mix, batch_index, groups, 0, 0.0).reshape(
            BEAMS, requests, heads_dev, head_part
        )
        chain_peak, chain_total, chain_weights = partial_softmax(
            chain_scores.reshape(BEAMS, requests, heads_dev, -1), chain_ok
        )
        chain_weights = chain_weights.reshape(BEAMS, requests, heads_dev, beam_dev, history + STEPS)
        chain_mix = jnp.einsum(
            "brnjt,jrtnd->brnd",
            chain_weights[..., :history],
            old_values,
            preferred_element_type=jnp.float32,
        )
        chain_mix = chain_mix + jnp.einsum(
            "brnjt,jrtnd->brnd",
            chain_weights[..., history:],
            stored_v,
            preferred_element_type=jnp.float32,
        )
        joined = combine((peak_full, total_full, mix_full), (chain_peak, chain_total, chain_mix))
        merged = joined_2((joined[0], joined[1], joined[2]), "batch", combine)
        first_beam = batch_index * beam_dev
        total_own = lax.dynamic_slice_in_dim(merged[1], first_beam, beam_dev, 0)
        mix_own = lax.dynamic_slice_in_dim(merged[2], first_beam, beam_dev, 0)
        attention = (
            (mix_own / total_own[..., None])
            .reshape(beam_dev, requests, columns)
            .astype(jnp.bfloat16)
        )
        summed = lax.psum_scatter(
            jnp.einsum("brc,cd->rbd", attention, out_weight, preferred_element_type=jnp.float32)
            + jnp.einsum("brf,fd->rbd", hidden, down_weight, preferred_element_type=jnp.float32),
            "tensor",
            scatter_dimension=0,
            tiled=True,
        )
        update = jnp.transpose(summed, (1, 0, 2))
        result = current.astype(jnp.float32) + update + down_bias
        outputs.append(result)
    return jnp.stack(outputs, axis=0)


VMEM_LIMIT = 58 * 2**20
EXTRA = 128


def dot32(a, b):
    return jnp.dot(a, b, preferred_element_type=jnp.float32)


def dot32_t(a, b):
    return lax.dot_general(a, b, (((1,), (1,)), ((), ())), preferred_element_type=jnp.float32)


def turn(tile, cosine, sine):
    lane = lax.broadcasted_iota(jnp.int32, tile.shape, 1)
    after = pltpu.roll(tile, HDIM - 1, 1)
    before = pltpu.roll(tile, 1, 1)
    return tile * cosine + jnp.where(lane % 2 == 0, after, before) * sine


def project_kernel(tiles, x_ref, qkv_ref, in_ref, bias_ref, cos_ref, sin_ref, q_ref, kv_ref, hid_ref):
    j = pl.program_id(0)

    @pl.when(j < 2 * tiles)
    def _():
        turned = turn(dot32(x_ref[...], qkv_ref[0]), cos_ref[...], sin_ref[...]).astype(jnp.bfloat16)

        @pl.when(j < tiles)
        def _():
            q_ref[...] = turned

        @pl.when(j >= tiles)
        def _():
            kv_ref[0] = turned

    @pl.when((j >= 2 * tiles) & (j < 3 * tiles))
    def _():
        kv_ref[0] = dot32(x_ref[...], qkv_ref[0]).astype(jnp.bfloat16)

    @pl.when(j >= 3 * tiles)
    def _():
        hid_ref[...] = jax.nn.gelu(
            dot32(x_ref[...], in_ref[...]) + bias_ref[...], approximate=True
        ).astype(jnp.bfloat16)


def project(rows, qkv3, in_weight, in_bias, cosine, sine):
    count, width = rows.shape
    columns = qkv3.shape[2]
    units = in_weight.shape[1]
    tiles = columns // HDIM
    steps = 3 * tiles + units // HDIM
    return pl.pallas_call(
        lambda *refs: project_kernel(tiles, *refs),
        grid=(steps,),
        in_specs=[
            pl.BlockSpec((count, width), lambda j: (0, 0)),
            pl.BlockSpec(
                (1, width, HDIM),
                lambda j: (
                    jnp.minimum(j, 3 * tiles - 1) // tiles,
                    0,
                    jnp.minimum(j, 3 * tiles - 1) % tiles,
                ),
            ),
            pl.BlockSpec((width, HDIM), lambda j: (0, jnp.maximum(j - 3 * tiles, 0))),
            pl.BlockSpec((1, HDIM), lambda j: (0, jnp.maximum(j - 3 * tiles, 0))),
            pl.BlockSpec((count, HDIM), lambda j: (0, 0)),
            pl.BlockSpec((count, HDIM), lambda j: (0, 0)),
        ],
        out_specs=[
            pl.BlockSpec((count, HDIM), lambda j: (0, jnp.minimum(j, tiles - 1))),
            pl.BlockSpec(
                (1, count, HDIM),
                lambda j: (
                    jnp.clip(j - tiles, 0, 2 * tiles - 1) // tiles,
                    0,
                    jnp.clip(j - tiles, 0, 2 * tiles - 1) % tiles,
                ),
            ),
            pl.BlockSpec((count, HDIM), lambda j: (0, jnp.maximum(j - 3 * tiles, 0))),
        ],
        out_shape=[
            jax.ShapeDtypeStruct((count, columns), jnp.bfloat16),
            jax.ShapeDtypeStruct((2, count, columns), jnp.bfloat16),
            jax.ShapeDtypeStruct((count, units), jnp.bfloat16),
        ],
        compiler_params=pltpu.CompilerParams(vmem_limit_bytes=VMEM_LIMIT),
    )(rows, qkv3, in_weight, in_bias.reshape(1, units), cosine, sine)


def attend_kernel(
    groups, beam_dev, heads, pages,
    table_ref, length_ref, place_ref,
    q_ref, kv_ref, old_ref, line_ref, *rest,
):
    page_refs = rest[:pages]
    out_ref, mix_ref, peak_ref, total_ref = rest[pages:]
    step = pl.program_id(0)
    place = place_ref[0]
    first = place * beam_dev
    rows = q_ref.shape[2]
    span = old_ref.shape[3]
    page = page_refs[0].shape[2]
    scale = HDIM ** (-0.5)

    def query_rows(j):
        parts = [q_ref[g, j].astype(jnp.float32) for g in range(groups)]
        return jnp.concatenate(parts, axis=0).astype(jnp.bfloat16)

    for j in range(groups):
        query = query_rows(j)
        line = line_ref[j]
        new_lane = lax.broadcasted_iota(jnp.int32, (groups * rows, rows), 1)
        new_ok = line[:, :rows] == first + new_lane % beam_dev
        root = line[:, rows : rows + 1]
        for h in range(heads):
            cols = slice(h * HDIM, (h + 1) * HDIM)
            scores = [
                dot32_t(query[:, cols], old_ref[i, j, 0, :, cols]) * scale for i in range(beam_dev)
            ]
            oks = [jnp.broadcast_to(root == first + i, scores[i].shape) for i in range(beam_dev)]
            scores.append(dot32_t(query[:, cols], kv_ref[0, j, :, cols]) * scale)
            oks.append(new_ok)
            values = [old_ref[i, j, 1, :, cols] for i in range(beam_dev)] + [kv_ref[1, j, :, cols]]
            masked = [jnp.where(ok, s, NEG_FILL) for ok, s in zip(oks, scores)]
            peak = masked[0].max(axis=1, keepdims=True)
            for m in masked[1:]:
                peak = jnp.maximum(peak, m.max(axis=1, keepdims=True))
            total = 0.0
            mix = 0.0
            for m, ok, v in zip(masked, oks, values):
                weights = jnp.where(ok, jnp.exp(m - peak), 0.0)
                total = total + weights.sum(axis=1, keepdims=True)
                mix = mix + dot32(weights.astype(jnp.bfloat16), v)
            mix_ref[j, :, cols] = mix
            peak_ref[j, h] = jnp.broadcast_to(peak, peak_ref.shape[2:])
            total_ref[j, h] = jnp.broadcast_to(total, total_ref.shape[2:])

    query = query_rows(place)
    for h in range(heads):
        cols = slice(h * HDIM, (h + 1) * HDIM)
        masked = []
        oks = []
        for p in range(pages):
            s = dot32_t(query[:, cols], page_refs[p][0, 0, :, cols]) * scale
            ok = lax.broadcasted_iota(jnp.int32, s.shape, 1) + p * page < length_ref[step]
            masked.append(jnp.where(ok, s, NEG_FILL))
            oks.append(ok)
        old_peak = peak_ref[place, h][:, :1]
        peak = old_peak
        for m in masked:
            peak = jnp.maximum(peak, m.max(axis=1, keepdims=True))
        factor = jnp.exp(old_peak - peak)
        total = total_ref[place, h][:, :1] * factor
        mix = mix_ref[place, :, cols] * factor
        for p in range(pages):
            weights = jnp.where(oks[p], jnp.exp(masked[p] - peak), 0.0)
            total = total + weights.sum(axis=1, keepdims=True)
            mix = mix + dot32(weights.astype(jnp.bfloat16), page_refs[p][0, 1, :, cols])
        mix_ref[place, :, cols] = mix
        peak_ref[place, h] = jnp.broadcast_to(peak, peak_ref.shape[2:])
        total_ref[place, h] = jnp.broadcast_to(total, total_ref.shape[2:])

    lane = lax.broadcasted_iota(jnp.int32, (groups * rows, EXTRA), 1)
    columns = heads * HDIM
    for j in range(groups):
        extra = jnp.zeros((groups * rows, EXTRA), jnp.float32)
        for h in range(heads):
            cols = slice(h * HDIM, (h + 1) * HDIM)
            total = total_ref[j, h]
            held = total > 0.0
            safe = jnp.where(held, total, 1.0)
            level = jnp.where(held, peak_ref[j, h] + jnp.log(safe), NEG_FILL)
            top = level.astype(jnp.bfloat16).astype(jnp.float32)
            middle = (level - top).astype(jnp.bfloat16).astype(jnp.float32)
            low = level - top - middle
            extra = jnp.where(lane == 3 * h, top, extra)
            extra = jnp.where(lane == 3 * h + 1, middle, extra)
            extra = jnp.where(lane == 3 * h + 2, low, extra)
            mixed = mix_ref[j, :, cols] / safe[:, :1]
            for g in range(groups):
                out_ref[g, j, :, cols] = mixed[g * rows : (g + 1) * rows].astype(jnp.bfloat16)
        for g in range(groups):
            out_ref[g, j, :, columns:] = extra[g * rows : (g + 1) * rows].astype(jnp.bfloat16)


def attend(query_all, kv, old_cache, line, page_pool, table, lengths, place):
    groups, requests, rows, columns = query_all.shape
    beam_dev, _, _, span, _ = old_cache.shape
    pages = table.shape[1]
    page = page_pool.shape[2]
    heads = columns // HDIM
    many = groups * rows

    def page_spec(p):
        return pl.BlockSpec(
            (1, 2, page, columns), lambda i, table, *_: (table[i * pages + p], 0, 0, 0)
        )

    return pl.pallas_call(
        lambda *refs: attend_kernel(groups, beam_dev, heads, pages, *refs),
        grid_spec=pltpu.PrefetchScalarGridSpec(
            num_scalar_prefetch=3,
            grid=(requests // groups,),
            in_specs=[
                pl.BlockSpec((groups, groups, rows, columns), lambda i, *_: (0, i, 0, 0)),
                pl.BlockSpec((2, groups, rows, columns), lambda i, *_: (0, i, 0, 0)),
                pl.BlockSpec((beam_dev, groups, 2, span, columns), lambda i, *_: (0, i, 0, 0, 0)),
                pl.BlockSpec((groups, many, line.shape[2]), lambda i, *_: (i, 0, 0)),
            ]
            + [page_spec(p) for p in range(pages)],
            out_specs=pl.BlockSpec(
                (groups, groups, rows, columns + EXTRA), lambda i, *_: (0, i, 0, 0)
            ),
            scratch_shapes=[
                pltpu.VMEM((groups, many, columns), jnp.float32),
                pltpu.VMEM((groups, heads, many, EXTRA), jnp.float32),
                pltpu.VMEM((groups, heads, many, EXTRA), jnp.float32),
            ],
        ),
        out_shape=jax.ShapeDtypeStruct((groups, requests, rows, columns + EXTRA), jnp.bfloat16),
        compiler_params=pltpu.CompilerParams(vmem_limit_bytes=VMEM_LIMIT),
    )(table.reshape(-1), lengths, place, query_all, kv, old_cache, line, *[page_pool] * pages)


def lineage_table(parents, groups, beam_dev):
    steps, beams, requests = parents.shape
    beam_ids = jnp.broadcast_to(jnp.arange(beams)[:, None], (beams, requests))
    every = []
    for step in range(steps):
        lineage = beam_ids
        found = []
        for back in range(step, -1, -1):
            found.append(lineage)
            hits = lineage[:, None, :] == jnp.arange(beams)[None, :, None]
            lineage = jnp.sum(jnp.where(hits, parents[back][None], 0), axis=1)
        found = found[::-1] + [jnp.full_like(beam_ids, -1)] * (steps - 1 - step)
        lanes = [f for f in found for _ in range(beam_dev)]
        every.append(jnp.stack(lanes + [lineage], axis=-1))
    table = jnp.stack(every, axis=0).reshape(steps, groups, beam_dev, requests, -1)
    table = jnp.transpose(table, (3, 1, 0, 2, 4))
    return table.reshape(requests, groups * steps * beam_dev, -1)


def rotary_tables(prompt_length, history, steps, beam_dev):
    requests = prompt_length.shape[0]
    lane = jnp.arange(HDIM)
    doubled = lane - lane % 2
    frequency = jnp.where(
        doubled < ROT, jnp.exp(-doubled.astype(jnp.float32) / ROT * math.log(10000.0)), 0.0
    )
    position = (prompt_length[:, None] + history + jnp.arange(steps)).astype(jnp.float32)
    angles = position[:, :, None] * frequency
    sign = jnp.where(lane % 2 == 0, -1.0, 1.0)
    shape = (requests, steps, beam_dev, HDIM)

    def spread(table):
        return jnp.broadcast_to(table[:, :, None], shape).reshape(-1, HDIM)

    return spread(jnp.cos(angles)), spread(jnp.sin(angles) * sign)


def together(
    inputs, norm_gain, norm_bias, qkv_weight, out_weight, in_weight, in_bias, down_weight,
    down_bias, page_pool, old_cache, page_table, prompt_length, parents,
):
    place = lax.axis_index("batch")
    groups = lax.axis_size("batch")
    tensors = lax.axis_size("tensor")
    steps, beam_dev, own_requests, width = inputs.shape
    requests, pages = page_table.shape
    columns = qkv_weight.shape[2]
    heads = columns // HDIM
    rows = steps * beam_dev
    cosine, sine = rotary_tables(prompt_length, old_cache.shape[3], steps, beam_dev)
    line = lineage_table(parents, groups, beam_dev)
    own = jnp.arange(requests // groups) * groups + place
    table = jnp.take(page_table, own, axis=0) - place * page_pool.shape[0]
    lengths = jnp.take(prompt_length, own, axis=0)
    current = jnp.transpose(inputs, (2, 0, 1, 3)).reshape(own_requests * rows, width)
    normed = normalize(current, norm_gain, norm_bias).astype(jnp.bfloat16)
    gathered = lax.all_gather(normed, "tensor", axis=0, tiled=True)
    query, kv, hidden = project(
        gathered, jnp.transpose(qkv_weight, (1, 0, 2)), in_weight, in_bias, cosine, sine
    )
    query_all = lax.all_gather(query, "batch").reshape(groups, requests, rows, columns)
    partial = attend(
        query_all, kv.reshape(2, requests, rows, columns), old_cache, line, page_pool, table,
        lengths, place[None],
    )
    landed = lax.all_to_all(
        partial.reshape(groups, requests * rows, columns + EXTRA), "batch", 0, 0
    )
    levels = landed[:, :, columns : columns + 3 * heads].astype(jnp.float32)
    levels = levels.reshape(groups, requests * rows, heads, 3).sum(axis=-1)
    shares = jnp.exp(levels - levels.max(axis=0))
    shares = shares / shares.sum(axis=0)
    attention = sum(
        landed[g, :, :columns].astype(jnp.float32) * jnp.repeat(shares[g], HDIM, axis=1)
        for g in range(groups)
    ).astype(jnp.bfloat16)
    update = dot32(attention, out_weight) + dot32(hidden, down_weight)
    update = update.astype(jnp.bfloat16).reshape(tensors, own_requests * rows, width)
    shared = lax.all_to_all(update, "tensor", 0, 0)
    result = current.astype(jnp.float32) + shared.astype(jnp.float32).sum(axis=0) + down_bias
    return jnp.transpose(result.reshape(own_requests, steps, beam_dev, width), (1, 2, 0, 3))


def on_device(*arrays):
    columns = arrays[3].shape[2]
    if columns % HDIM:
        return stepwise(*arrays)
    return together(*arrays)


def solution(mesh):
    in_specs = (
        P(None, "batch", "tensor", None),
        P(),
        P(),
        P(None, None, "tensor"),
        P("tensor", None),
        P(None, "tensor"),
        P("tensor"),
        P("tensor", None),
        P(),
        P("batch", None, None, "tensor"),
        P("batch", None, None, None, "tensor"),
        P(),
        P(),
        P(),
    )
    out_specs = P(None, "batch", "tensor", None)
    return jax.shard_map(
        on_device, mesh=mesh, in_specs=in_specs, out_specs=out_specs, check_vma=False
    )
```

```python
import math

import jax
import jax.numpy as jnp
from jax import lax
from jax.experimental import pallas as pl
from jax.experimental.pallas import tpu as pltpu
from jax.sharding import PartitionSpec as P

HDIM = 256
ROT = 64
BEAMS = 8
STEPS = 4


NEG_FILL = -1e30


def partner(value, axis, bit):
    return lax.ppermute(value, axis, [(i, i ^ 1 << bit) for i in range(lax.axis_size(axis))])


def joined_2(part, axis, combine):
    gathered = jax.tree.map(lambda a: lax.all_gather(a, axis), part)

    def take(source):
        return jax.tree.map(lambda a: lax.dynamic_index_in_dim(a, source, 0, False), gathered)

    return lax.fori_loop(
        1, lax.axis_size(axis), lambda source, state: combine(state, take(source)), take(0)
    )


def normalize(row_block, norm_gain, norm_bias):
    widened = row_block.astype(jnp.float32)
    center = jnp.mean(widened, axis=-1, keepdims=True)
    shifted = widened - center
    variance = jnp.mean(shifted * shifted, axis=-1, keepdims=True)
    return shifted * lax.rsqrt(variance + 1e-05) * norm_gain + norm_bias


def rotate_local(vectors, position, first_column):
    half_count = vectors.shape[-1] // 2
    doubled = (first_column + 2 * jnp.arange(half_count)) % HDIM
    exponent = doubled.astype(jnp.float32) / ROT
    frequency = jnp.where(doubled < ROT, jnp.exp(-exponent * math.log(10000.0)), 0.0)
    angles = position[:, None] * frequency[None, :]
    cosine = jnp.cos(angles)[None]
    sine_part = jnp.sin(angles)[None]
    halves = vectors.reshape(vectors.shape[:-1] + (half_count, 2))
    even_part = halves[..., 0]
    odd_part = halves[..., 1]
    turned = jnp.stack(
        [even_part * cosine - odd_part * sine_part, odd_part * cosine + even_part * sine_part],
        axis=-1,
    )
    return turned.reshape(vectors.shape)


def combine(earlier, later):
    peak_one, total_one, mixture_one = earlier
    peak_two, total_two, mixture_two = later
    peak = jnp.maximum(peak_one, peak_two)
    factor_one = jnp.exp(peak_one - peak)
    factor_two = jnp.exp(peak_two - peak)
    return (
        peak,
        total_one * factor_one + total_two * factor_two,
        mixture_one * factor_one[..., None] + mixture_two * factor_two[..., None],
    )


def partial_softmax(scores, allowed):
    masked = jnp.where(allowed, scores, NEG_FILL)
    peak = jnp.max(masked, axis=-1)
    weights = jnp.where(allowed, jnp.exp(masked - peak[..., None]), 0.0)
    return (peak, jnp.sum(weights, axis=-1), weights.astype(jnp.bfloat16))


def place_block(values, slot, slot_count, axis, fill_value):
    hit_shape = [1] * (values.ndim + 1)
    hit_shape[axis] = slot_count
    hits = (jnp.arange(slot_count) == slot).reshape(hit_shape)
    return jnp.where(hits, jnp.expand_dims(values, axis), fill_value)


def head_sum(prompt_scores, chain_scores, spread):
    for bit_index in range(spread.bit_length() - 1):
        other_prompt, other_chain = partner((prompt_scores, chain_scores), "tensor", bit_index)
        prompt_scores = prompt_scores + other_prompt
        chain_scores = chain_scores + other_chain
    return (prompt_scores, chain_scores)


def stepwise(
    inputs,
    norm_gain,
    norm_bias,
    qkv_weight,
    out_weight,
    in_weight,
    in_bias,
    down_weight,
    down_bias,
    page_pool,
    old_cache,
    page_table,
    prompt_length,
    parents,
):
    batch_index = lax.axis_index("batch")
    tensor_index = lax.axis_index("tensor")
    groups = lax.axis_size("batch")
    beam_dev = inputs.shape[1]
    model_width = inputs.shape[3]
    columns = qkv_weight.shape[2]
    requests = page_table.shape[0]
    history = old_cache.shape[3]
    prompt_span = page_table.shape[1] * page_pool.shape[2]
    heads_dev = max(columns // HDIM, 1)
    head_part = min(columns, HDIM)
    spread = max(HDIM // columns, 1)
    scale_factor = HDIM ** (-0.5)
    qkv_flat = qkv_weight.reshape(model_width, 3 * columns)
    first_column = tensor_index * columns
    owners = batch_index * beam_dev + jnp.arange(beam_dev)
    old_keys = old_cache[:, :, 0].reshape(beam_dev, requests, history, heads_dev, head_part)
    old_values = old_cache[:, :, 1].reshape(beam_dev, requests, history, heads_dev, head_part)
    stored_keys = jnp.zeros((beam_dev, requests, STEPS, columns), jnp.bfloat16)
    stored_values = jnp.zeros((beam_dev, requests, STEPS, columns), jnp.bfloat16)
    beam_ids = jnp.broadcast_to(jnp.arange(BEAMS)[:, None], (BEAMS, requests))
    prompt_ok = jnp.arange(prompt_span)[None, :] < prompt_length[:, None]
    whole_pool = lax.all_gather(page_pool, "batch", axis=0, tiled=True)
    page_rows = whole_pool[page_table]
    count_rows = page_table.shape[0]
    prompt_keys = page_rows[:, :, 0].reshape(count_rows, prompt_span, heads_dev, head_part)
    prompt_values = page_rows[:, :, 1].reshape(count_rows, prompt_span, heads_dev, head_part)
    outputs = []
    for step_index in range(STEPS):
        current = inputs[step_index]
        normed = normalize(current, norm_gain, norm_bias).astype(jnp.bfloat16)
        gathered_rows = lax.all_gather(normed, "tensor", axis=1, tiled=True)
        attn_part = jnp.einsum(
            "brd,dc->brc", gathered_rows, qkv_flat, preferred_element_type=jnp.float32
        )
        ffn_part = jnp.einsum(
            "brd,dc->brc", gathered_rows, in_weight, preferred_element_type=jnp.float32
        )
        projected = jnp.concatenate([attn_part, ffn_part], axis=-1)
        position = (prompt_length + history + step_index).astype(jnp.float32)
        queries = rotate_local(projected[..., :columns], position, first_column).astype(
            jnp.bfloat16
        )
        fresh_keys = rotate_local(
            projected[..., columns : 2 * columns], position, first_column
        ).astype(jnp.bfloat16)
        fresh_values = projected[..., 2 * columns : 3 * columns].astype(jnp.bfloat16)
        hidden = jax.nn.gelu(projected[..., 3 * columns :] + in_bias, approximate=True).astype(
            jnp.bfloat16
        )
        stored_keys = stored_keys.at[:, :, step_index].set(fresh_keys)
        stored_values = stored_values.at[:, :, step_index].set(fresh_values)
        queries_all = lax.all_gather(queries, "batch", axis=0, tiled=True)
        query_heads = queries_all.reshape(BEAMS, requests, heads_dev, head_part)
        own_heads = queries.reshape(beam_dev, requests, heads_dev, head_part)
        ancestry = []
        lineage = beam_ids
        for back_step in range(step_index, -1, -1):
            ancestry.append(lineage)
            lineage = jnp.take_along_axis(parents[back_step], lineage, axis=0)
        unused_steps = [jnp.full_like(beam_ids, -1)] * (STEPS - 1 - step_index)
        ancestry_all = jnp.stack(ancestry[::-1] + unused_steps, axis=-1)
        stored_k = stored_keys.reshape(beam_dev, requests, STEPS, heads_dev, head_part)
        stored_v = stored_values.reshape(beam_dev, requests, STEPS, heads_dev, head_part)
        chain_scores = (
            jnp.concatenate(
                [
                    jnp.einsum(
                        "brnd,jrtnd->brnjt",
                        query_heads,
                        old_keys,
                        preferred_element_type=jnp.float32,
                    ),
                    jnp.einsum(
                        "brnd,jrtnd->brnjt",
                        query_heads,
                        stored_k,
                        preferred_element_type=jnp.float32,
                    ),
                ],
                axis=-1,
            )
            * scale_factor
        )
        old_ok = jnp.broadcast_to(
            (lineage[:, :, None] == owners[None, None, :])[:, :, :, None],
            (BEAMS, requests, beam_dev, history),
        )
        new_ok = ancestry_all[:, :, None, :] == owners[None, None, :, None]
        chain_ok = jnp.concatenate([old_ok, new_ok], axis=-1).reshape(BEAMS, requests, 1, -1)
        prompt_scores = (
            jnp.einsum(
                "brnd,rtnd->brnt", own_heads, prompt_keys, preferred_element_type=jnp.float32
            )
            * scale_factor
        )
        prompt_scores, chain_scores = head_sum(prompt_scores, chain_scores, spread)
        prompt_peak, prompt_total, prompt_weights = partial_softmax(
            prompt_scores, prompt_ok[None, :, None, :]
        )
        prompt_mix = jnp.einsum(
            "brnt,rtnd->brnd", prompt_weights, prompt_values, preferred_element_type=jnp.float32
        )
        peak_full = place_block(prompt_peak, batch_index, groups, 0, NEG_FILL).reshape(
            BEAMS, requests, heads_dev
        )
        total_full = place_block(prompt_total, batch_index, groups, 0, 0.0).reshape(
            BEAMS, requests, heads_dev
        )
        mix_full = place_block(prompt_mix, batch_index, groups, 0, 0.0).reshape(
            BEAMS, requests, heads_dev, head_part
        )
        chain_peak, chain_total, chain_weights = partial_softmax(
            chain_scores.reshape(BEAMS, requests, heads_dev, -1), chain_ok
        )
        chain_weights = chain_weights.reshape(BEAMS, requests, heads_dev, beam_dev, history + STEPS)
        chain_mix = jnp.einsum(
            "brnjt,jrtnd->brnd",
            chain_weights[..., :history],
            old_values,
            preferred_element_type=jnp.float32,
        )
        chain_mix = chain_mix + jnp.einsum(
            "brnjt,jrtnd->brnd",
            chain_weights[..., history:],
            stored_v,
            preferred_element_type=jnp.float32,
        )
        joined = combine((peak_full, total_full, mix_full), (chain_peak, chain_total, chain_mix))
        merged = joined_2((joined[0], joined[1], joined[2]), "batch", combine)
        first_beam = batch_index * beam_dev
        total_own = lax.dynamic_slice_in_dim(merged[1], first_beam, beam_dev, 0)
        mix_own = lax.dynamic_slice_in_dim(merged[2], first_beam, beam_dev, 0)
        attention = (
            (mix_own / total_own[..., None])
            .reshape(beam_dev, requests, columns)
            .astype(jnp.bfloat16)
        )
        summed = lax.psum_scatter(
            jnp.einsum("brc,cd->rbd", attention, out_weight, preferred_element_type=jnp.float32)
            + jnp.einsum("brf,fd->rbd", hidden, down_weight, preferred_element_type=jnp.float32),
            "tensor",
            scatter_dimension=0,
            tiled=True,
        )
        update = jnp.transpose(summed, (1, 0, 2))
        result = current.astype(jnp.float32) + update + down_bias
        outputs.append(result)
    return jnp.stack(outputs, axis=0)


VMEM_LIMIT = 58 * 2**20
EXTRA = 128


def dot32(a, b):
    return jnp.dot(a, b, preferred_element_type=jnp.float32)


def dot32_t(a, b):
    return lax.dot_general(a, b, (((1,), (1,)), ((), ())), preferred_element_type=jnp.float32)


def turn(tile, cosine, sine):
    lane = lax.broadcasted_iota(jnp.int32, tile.shape, 1)
    after = pltpu.roll(tile, HDIM - 1, 1)
    before = pltpu.roll(tile, 1, 1)
    return tile * cosine + jnp.where(lane % 2 == 0, after, before) * sine


def project_kernel(tiles, x_ref, qkv_ref, in_ref, bias_ref, cos_ref, sin_ref, q_ref, kv_ref, hid_ref):
    j = pl.program_id(0)

    @pl.when(j < 2 * tiles)
    def _():
        turned = turn(dot32(x_ref[...], qkv_ref[0]), cos_ref[...], sin_ref[...]).astype(jnp.bfloat16)

        @pl.when(j < tiles)
        def _():
            q_ref[...] = turned

        @pl.when(j >= tiles)
        def _():
            kv_ref[0] = turned

    @pl.when((j >= 2 * tiles) & (j < 3 * tiles))
    def _():
        kv_ref[0] = dot32(x_ref[...], qkv_ref[0]).astype(jnp.bfloat16)

    @pl.when(j >= 3 * tiles)
    def _():
        hid_ref[...] = jax.nn.gelu(
            dot32(x_ref[...], in_ref[...]) + bias_ref[...], approximate=True
        ).astype(jnp.bfloat16)


def project(rows, qkv3, in_weight, in_bias, cosine, sine):
    count, width = rows.shape
    columns = qkv3.shape[2]
    units = in_weight.shape[1]
    tiles = columns // HDIM
    steps = 3 * tiles + units // HDIM
    return pl.pallas_call(
        lambda *refs: project_kernel(tiles, *refs),
        grid=(steps,),
        in_specs=[
            pl.BlockSpec((count, width), lambda j: (0, 0)),
            pl.BlockSpec(
                (1, width, HDIM),
                lambda j: (
                    jnp.minimum(j, 3 * tiles - 1) // tiles,
                    0,
                    jnp.minimum(j, 3 * tiles - 1) % tiles,
                ),
            ),
            pl.BlockSpec((width, HDIM), lambda j: (0, jnp.maximum(j - 3 * tiles, 0))),
            pl.BlockSpec((1, HDIM), lambda j: (0, jnp.maximum(j - 3 * tiles, 0))),
            pl.BlockSpec((count, HDIM), lambda j: (0, 0)),
            pl.BlockSpec((count, HDIM), lambda j: (0, 0)),
        ],
        out_specs=[
            pl.BlockSpec((count, HDIM), lambda j: (0, jnp.minimum(j, tiles - 1))),
            pl.BlockSpec(
                (1, count, HDIM),
                lambda j: (
                    jnp.clip(j - tiles, 0, 2 * tiles - 1) // tiles,
                    0,
                    jnp.clip(j - tiles, 0, 2 * tiles - 1) % tiles,
                ),
            ),
            pl.BlockSpec((count, HDIM), lambda j: (0, jnp.maximum(j - 3 * tiles, 0))),
        ],
        out_shape=[
            jax.ShapeDtypeStruct((count, columns), jnp.bfloat16),
            jax.ShapeDtypeStruct((2, count, columns), jnp.bfloat16),
            jax.ShapeDtypeStruct((count, units), jnp.bfloat16),
        ],
        compiler_params=pltpu.CompilerParams(vmem_limit_bytes=VMEM_LIMIT),
    )(rows, qkv3, in_weight, in_bias.reshape(1, units), cosine, sine)


def attend_kernel(
    groups, beam_dev, heads, pages,
    table_ref, length_ref, place_ref,
    q_ref, kv_ref, old_ref, line_ref, *rest,
):
    page_refs = rest[:pages]
    out_ref, mix_ref, peak_ref, total_ref = rest[pages:]
    step = pl.program_id(0)
    place = place_ref[0]
    first = place * beam_dev
    rows = q_ref.shape[2]
    span = old_ref.shape[3]
    page = page_refs[0].shape[2]
    scale = HDIM ** (-0.5)
    old_lane = lax.broadcasted_iota(jnp.int32, (groups * rows, beam_dev * span), 1)

    def query_rows(j):
        parts = [q_ref[g, j].astype(jnp.float32) for g in range(groups)]
        return jnp.concatenate(parts, axis=0).astype(jnp.bfloat16)

    for j in range(groups):
        query = query_rows(j)
        line = line_ref[j]
        new_lane = lax.broadcasted_iota(jnp.int32, (groups * rows, rows), 1)
        new_ok = line[:, :rows] == first + new_lane % beam_dev
        root = line[:, rows : rows + 1]
        for h in range(heads):
            cols = slice(h * HDIM, (h + 1) * HDIM)
            old_keys = jnp.concatenate(
                [old_ref[i, j, 0, :, cols] for i in range(beam_dev)], axis=0
            )
            old_values = jnp.concatenate(
                [old_ref[i, j, 1, :, cols] for i in range(beam_dev)], axis=0
            )
            scores = [
                dot32_t(query[:, cols], old_keys) * scale,
                dot32_t(query[:, cols], kv_ref[0, j, :, cols]) * scale,
            ]
            oks = [root == first + old_lane // span, new_ok]
            values = [old_values, kv_ref[1, j, :, cols]]
            masked = [jnp.where(ok, s, NEG_FILL) for ok, s in zip(oks, scores)]
            peak = masked[0].max(axis=1, keepdims=True)
            for m in masked[1:]:
                peak = jnp.maximum(peak, m.max(axis=1, keepdims=True))
            total = 0.0
            mix = 0.0
            for m, ok, v in zip(masked, oks, values):
                weights = jnp.where(ok, jnp.exp(m - peak), 0.0)
                total = total + weights.sum(axis=1, keepdims=True)
                mix = mix + dot32(weights.astype(jnp.bfloat16), v)
            mix_ref[j, :, cols] = mix
            peak_ref[j, h] = jnp.broadcast_to(peak, peak_ref.shape[2:])
            total_ref[j, h] = jnp.broadcast_to(total, total_ref.shape[2:])

    query = query_rows(place)
    for h in range(heads):
        cols = slice(h * HDIM, (h + 1) * HDIM)
        masked = []
        oks = []
        for p in range(pages):
            s = dot32_t(query[:, cols], page_refs[p][0, 0, :, cols]) * scale
            ok = lax.broadcasted_iota(jnp.int32, s.shape, 1) + p * page < length_ref[step]
            masked.append(jnp.where(ok, s, NEG_FILL))
            oks.append(ok)
        old_peak = peak_ref[place, h][:, :1]
        peak = old_peak
        for m in masked:
            peak = jnp.maximum(peak, m.max(axis=1, keepdims=True))
        factor = jnp.exp(old_peak - peak)
        total = total_ref[place, h][:, :1] * factor
        mix = mix_ref[place, :, cols] * factor
        for p in range(pages):
            weights = jnp.where(oks[p], jnp.exp(masked[p] - peak), 0.0)
            total = total + weights.sum(axis=1, keepdims=True)
            mix = mix + dot32(weights.astype(jnp.bfloat16), page_refs[p][0, 1, :, cols])
        mix_ref[place, :, cols] = mix
        peak_ref[place, h] = jnp.broadcast_to(peak, peak_ref.shape[2:])
        total_ref[place, h] = jnp.broadcast_to(total, total_ref.shape[2:])

    lane = lax.broadcasted_iota(jnp.int32, (groups * rows, EXTRA), 1)
    columns = heads * HDIM
    for j in range(groups):
        extra = jnp.zeros((groups * rows, EXTRA), jnp.float32)
        for h in range(heads):
            cols = slice(h * HDIM, (h + 1) * HDIM)
            total = total_ref[j, h]
            held = total > 0.0
            safe = jnp.where(held, total, 1.0)
            level = jnp.where(held, peak_ref[j, h] + jnp.log(safe), NEG_FILL)
            top = level.astype(jnp.bfloat16).astype(jnp.float32)
            middle = (level - top).astype(jnp.bfloat16).astype(jnp.float32)
            low = level - top - middle
            extra = jnp.where(lane == 3 * h, top, extra)
            extra = jnp.where(lane == 3 * h + 1, middle, extra)
            extra = jnp.where(lane == 3 * h + 2, low, extra)
            mixed = mix_ref[j, :, cols] / safe[:, :1]
            for g in range(groups):
                out_ref[g, j, :, cols] = mixed[g * rows : (g + 1) * rows].astype(jnp.bfloat16)
        for g in range(groups):
            out_ref[g, j, :, columns:] = extra[g * rows : (g + 1) * rows].astype(jnp.bfloat16)


def attend(query_all, kv, old_cache, line, page_pool, table, lengths, place):
    groups, requests, rows, columns = query_all.shape
    beam_dev, _, _, span, _ = old_cache.shape
    pages = table.shape[1]
    page = page_pool.shape[2]
    heads = columns // HDIM
    many = groups * rows

    def page_spec(p):
        return pl.BlockSpec(
            (1, 2, page, columns), lambda i, table, *_: (table[i * pages + p], 0, 0, 0)
        )

    return pl.pallas_call(
        lambda *refs: attend_kernel(groups, beam_dev, heads, pages, *refs),
        grid_spec=pltpu.PrefetchScalarGridSpec(
            num_scalar_prefetch=3,
            grid=(requests // groups,),
            in_specs=[
                pl.BlockSpec((groups, groups, rows, columns), lambda i, *_: (0, i, 0, 0)),
                pl.BlockSpec((2, groups, rows, columns), lambda i, *_: (0, i, 0, 0)),
                pl.BlockSpec((beam_dev, groups, 2, span, columns), lambda i, *_: (0, i, 0, 0, 0)),
                pl.BlockSpec((groups, many, line.shape[2]), lambda i, *_: (i, 0, 0)),
            ]
            + [page_spec(p) for p in range(pages)],
            out_specs=pl.BlockSpec(
                (groups, groups, rows, columns + EXTRA), lambda i, *_: (0, i, 0, 0)
            ),
            scratch_shapes=[
                pltpu.VMEM((groups, many, columns), jnp.float32),
                pltpu.VMEM((groups, heads, many, EXTRA), jnp.float32),
                pltpu.VMEM((groups, heads, many, EXTRA), jnp.float32),
            ],
        ),
        out_shape=jax.ShapeDtypeStruct((groups, requests, rows, columns + EXTRA), jnp.bfloat16),
        compiler_params=pltpu.CompilerParams(vmem_limit_bytes=VMEM_LIMIT),
    )(table.reshape(-1), lengths, place, query_all, kv, old_cache, line, *[page_pool] * pages)


def peers(axis):
    count = lax.axis_size(axis)
    me = lax.axis_index(axis)
    beside = me + 1 - 2 * lax.rem(me, 2)
    ahead = [lax.rem(me + 2 * k, count) for k in range(count // 2)]
    behind = [lax.rem(me + count - 2 * k, count) for k in range(count // 2)]
    return me, beside, ahead, behind


def greet(axis, others):
    barrier = pltpu.get_barrier_semaphore()
    for other in others:
        pl.semaphore_signal(
            barrier, inc=1, device_id={axis: other}, device_id_type=pl.DeviceIdType.MESH
        )
    pl.semaphore_wait(barrier, len(others))


def remote(axis, source, target, sent, landed, other):
    return pltpu.make_async_remote_copy(
        src_ref=source,
        dst_ref=target,
        send_sem=sent,
        recv_sem=landed,
        device_id={axis: other},
        device_id_type=pl.DeviceIdType.MESH,
    )


def spread_kernel(axis, x_ref, out_ref, send_sem, land_sem, pass_sem, got_sem):
    me, beside, ahead, behind = peers(axis)
    half = len(ahead)
    greet(axis, [beside] + ahead[1:])
    sends = []
    for k in range(1, half):
        copy = remote(axis, x_ref, out_ref.at[me], send_sem.at[k], land_sem.at[k], ahead[k])
        copy.start()
        sends.append(copy)
    passes = [remote(axis, x_ref, out_ref.at[me], pass_sem.at[0], got_sem.at[0], beside)]
    passes[0].start()
    out_ref[me] = x_ref[...]
    for k in range(1, half):
        sends[k - 1].wait_recv()
        block = out_ref.at[behind[k]]
        copy = remote(axis, block, block, pass_sem.at[k], got_sem.at[k], beside)
        copy.start()
        passes.append(copy)
    for copy in passes:
        copy.wait_recv()
    for copy in sends + passes:
        copy.wait_send()


def spread_rows(block, axis, number):
    count = lax.axis_size(axis)
    return pl.pallas_call(
        lambda *refs: spread_kernel(axis, *refs),
        out_shape=jax.ShapeDtypeStruct((count,) + block.shape, block.dtype),
        in_specs=[pl.BlockSpec(memory_space=pltpu.VMEM)],
        out_specs=pl.BlockSpec(memory_space=pltpu.VMEM),
        scratch_shapes=[pltpu.SemaphoreType.DMA((count // 2,))] * 4,
        compiler_params=pltpu.CompilerParams(
            collective_id=number, has_side_effects=True, vmem_limit_bytes=VMEM_LIMIT
        ),
    )(block)


def total_kernel(
    axis, part_ref, current_ref, bias_ref, out_ref, beside_ref, pair_ref, far_ref,
    pass_sem, got_sem, send_sem, land_sem,
):
    me, beside, ahead, _ = peers(axis)
    half = len(ahead)
    count = lax.axis_size(axis)
    greet(axis, [beside] + ahead[1:])
    order = list(range(1, half)) + [0]
    passes = {}
    for k in order:
        chunk = part_ref.at[lax.rem(beside + 2 * k, count)]
        passes[k] = remote(axis, chunk, beside_ref.at[k], pass_sem.at[k], got_sem.at[k], beside)
        passes[k].start()
    sends = {}
    for k in range(1, half):
        passes[k].wait_recv()
        pair = part_ref[ahead[k]].astype(jnp.float32) + beside_ref[k].astype(jnp.float32)
        pair_ref[k] = pair.astype(pair_ref.dtype)
        sends[k] = remote(
            axis, pair_ref.at[k], far_ref.at[k], send_sem.at[k], land_sem.at[k], ahead[k]
        )
        sends[k].start()
    passes[0].wait_recv()
    out_ref[...] = (
        part_ref[me].astype(jnp.float32)
        + beside_ref[0].astype(jnp.float32)
        + current_ref[...].astype(jnp.float32)
        + bias_ref[...]
    )
    for k in range(1, half):
        sends[k].wait_recv()
        out_ref[...] += far_ref[k].astype(jnp.float32)
    for k in order:
        passes[k].wait_send()
    for k in range(1, half):
        sends[k].wait_send()


def total_rows(parts, current, bias, axis, number):
    count, rows, width = parts.shape
    half = count // 2
    return pl.pallas_call(
        lambda *refs: total_kernel(axis, *refs),
        out_shape=jax.ShapeDtypeStruct((rows, width), jnp.float32),
        in_specs=[pl.BlockSpec(memory_space=pltpu.VMEM)] * 3,
        out_specs=pl.BlockSpec(memory_space=pltpu.VMEM),
        scratch_shapes=[pltpu.VMEM((half, rows, width), jnp.bfloat16)] * 3
        + [pltpu.SemaphoreType.DMA((half,))] * 4,
        compiler_params=pltpu.CompilerParams(
            collective_id=number, has_side_effects=True, vmem_limit_bytes=VMEM_LIMIT
        ),
    )(parts, current, bias.reshape(1, width))


def lineage_table(parents, groups, beam_dev):
    steps, beams, requests = parents.shape
    beam_ids = jnp.broadcast_to(jnp.arange(beams)[:, None], (beams, requests))
    every = []
    for step in range(steps):
        lineage = beam_ids
        found = []
        for back in range(step, -1, -1):
            found.append(lineage)
            hits = lineage[:, None, :] == jnp.arange(beams)[None, :, None]
            lineage = jnp.sum(jnp.where(hits, parents[back][None], 0), axis=1)
        found = found[::-1] + [jnp.full_like(beam_ids, -1)] * (steps - 1 - step)
        lanes = [f for f in found for _ in range(beam_dev)]
        every.append(jnp.stack(lanes + [lineage], axis=-1))
    table = jnp.stack(every, axis=0).reshape(steps, groups, beam_dev, requests, -1)
    table = jnp.transpose(table, (3, 1, 0, 2, 4))
    return table.reshape(requests, groups * steps * beam_dev, -1)


def rotary_tables(prompt_length, history, steps, beam_dev):
    requests = prompt_length.shape[0]
    lane = jnp.arange(HDIM)
    doubled = lane - lane % 2
    frequency = jnp.where(
        doubled < ROT, jnp.exp(-doubled.astype(jnp.float32) / ROT * math.log(10000.0)), 0.0
    )
    position = (prompt_length[:, None] + history + jnp.arange(steps)).astype(jnp.float32)
    angles = position[:, :, None] * frequency
    sign = jnp.where(lane % 2 == 0, -1.0, 1.0)
    shape = (requests, steps, beam_dev, HDIM)

    def spread(table):
        return jnp.broadcast_to(table[:, :, None], shape).reshape(-1, HDIM)

    return spread(jnp.cos(angles)), spread(jnp.sin(angles) * sign)


def together(
    inputs, norm_gain, norm_bias, qkv_weight, out_weight, in_weight, in_bias, down_weight,
    down_bias, page_pool, old_cache, page_table, prompt_length, parents,
):
    place = lax.axis_index("batch")
    groups = lax.axis_size("batch")
    tensors = lax.axis_size("tensor")
    steps, beam_dev, own_requests, width = inputs.shape
    requests, pages = page_table.shape
    columns = qkv_weight.shape[2]
    heads = columns // HDIM
    rows = steps * beam_dev
    cosine, sine = rotary_tables(prompt_length, old_cache.shape[3], steps, beam_dev)
    line = lineage_table(parents, groups, beam_dev)
    own = jnp.arange(requests // groups) * groups + place
    table = jnp.take(page_table, own, axis=0) - place * page_pool.shape[0]
    lengths = jnp.take(prompt_length, own, axis=0)
    current = jnp.transpose(inputs, (2, 0, 1, 3)).reshape(own_requests * rows, width)
    normed = normalize(current, norm_gain, norm_bias).astype(jnp.bfloat16)
    gathered = spread_rows(normed, "tensor", 0).reshape(requests * rows, width)
    query, kv, hidden = project(
        gathered, jnp.transpose(qkv_weight, (1, 0, 2)), in_weight, in_bias, cosine, sine
    )
    query_all = spread_rows(query, "batch", 1).reshape(groups, requests, rows, columns)
    partial = attend(
        query_all, kv.reshape(2, requests, rows, columns), old_cache, line, page_pool, table,
        lengths, place[None],
    )
    landed = lax.all_to_all(
        partial.reshape(groups, requests * rows, columns + EXTRA), "batch", 0, 0
    )
    levels = landed[:, :, columns : columns + 3 * heads].astype(jnp.float32)
    levels = levels.reshape(groups, requests * rows, heads, 3).sum(axis=-1)
    shares = jnp.exp(levels - levels.max(axis=0))
    shares = shares / shares.sum(axis=0)
    attention = sum(
        landed[g, :, :columns].astype(jnp.float32) * jnp.repeat(shares[g], HDIM, axis=1)
        for g in range(groups)
    ).astype(jnp.bfloat16)
    update = dot32(attention, out_weight) + dot32(hidden, down_weight)
    update = update.astype(jnp.bfloat16).reshape(tensors, own_requests * rows, width)
    result = total_rows(update, current, down_bias, "tensor", 2)
    return jnp.transpose(result.reshape(own_requests, steps, beam_dev, width), (1, 2, 0, 3))


def on_device(*arrays):
    columns = arrays[3].shape[2]
    if columns % HDIM or lax.axis_size("tensor") % 2 or lax.axis_size("batch") % 2:
        return stepwise(*arrays)
    return together(*arrays)


def solution(mesh):
    in_specs = (
        P(None, "batch", "tensor", None),
        P(),
        P(),
        P(None, None, "tensor"),
        P("tensor", None),
        P(None, "tensor"),
        P("tensor"),
        P("tensor", None),
        P(),
        P("batch", None, None, "tensor"),
        P("batch", None, None, None, "tensor"),
        P(),
        P(),
        P(),
    )
    out_specs = P(None, "batch", "tensor", None)
    return jax.shard_map(
        on_device, mesh=mesh, in_specs=in_specs, out_specs=out_specs, check_vma=False
    )
```
